256 devices in a mesh: seq: 128 (over y, x_lo, z, core), tp: 2 (over x_hi).
Axes of the slice: x: 4 (x_hi: 2, x_lo: 2; x = x_hi * 2 + x_lo), y: 4, z: 8, core: 2. Of those that a mesh axis runs over, the one named last changes fastest.
Arguments:
- activations: bfloat16 [32768, 8192], P('seq', 'tp'), may hold values from -400 to 400
- norm_gain: float32 [8192], P('tp'), may hold values from 0.25 to 1.75
- gate_values: bfloat16 [32768, 8192], P('seq', 'tp'), may hold values from -0.5 to 2
- se_filter: float32 [7, 8192], P(None, 'tp'), may hold values from -0.2 to 1
- mr_filter: bfloat16 [128, 8192], P(None, 'tp'), may hold values from -0.4 to 0.4
- band_offsets: int32 [64], P('tp'), may hold values from 0 to 1, as said below
- cotangent: bfloat16 [32768, 8192], P('seq', 'tp'), may hold values from -5 to 5
Outputs:
- output: bfloat16 [32768, 8192], P('seq', 'tp')
- input_grad: bfloat16 [32768, 8192], P('seq', 'tp')
- gain_grad: float32 [8192], P('tp')
- se_grad: float32 [7, 8192], P(None, 'tp')
- mr_grad: bfloat16 [128, 8192], P(None, 'tp')
The draws below stay inside these ranges and needn't reach their ends.
Inputs may be any that keep to these rules, and one draw needn't show every extreme that they name: `band_offsets`: exactly half of the 64 groups have offset 1.
All inputs are finite; a program needn't handle non-finite values.
Results may differ from the reference program's by a relative error of at most 0.0054.
Values may be sent and summed in bfloat16 or wider, within the bound.
A program may use at most 128 MiB of HBM per device.

```python
import math
import jax
import jax.numpy as jnp
from jax import lax

D = 8192
TAPS = 128
SE_TAPS = 7
GROUP = 128
TOKENS = 32768
GROUPS = 64


def draw_activations(key, part):
    key = jax.random.fold_in(key, 11)
    key_base, key_rows, key_cols = jax.random.split(key, 3)
    base = jax.random.truncated_normal(key_base, -3.5, 3.5, (TOKENS, D), jnp.float32)
    row_scale = jnp.exp(jax.random.uniform(key_rows, (TOKENS, 1), jnp.float32) * math.log(10.0))
    col_scale = jnp.exp(jax.random.uniform(key_cols, (1, D), jnp.float32) * math.log(10.0))
    return ((base + 0.3) * row_scale * col_scale).astype(jnp.bfloat16)


def draw_mr_filter(key, part):
    key = jax.random.fold_in(key, 12)
    key_base, key_rate = jax.random.split(key, 2)
    base = jax.random.truncated_normal(key_base, -3.4, 3.4, (TAPS, D), jnp.float32)
    rates = jnp.exp(jax.random.uniform(key_rate, (1, D), jnp.float32, math.log(0.001), math.log(0.06)))
    position = jnp.arange(TAPS, dtype=jnp.float32)[:, None]
    return (0.1 * (base + 0.6) * jnp.exp(-rates * position)).astype(jnp.bfloat16)


def draw_band_offsets(key, part):
    key = jax.random.fold_in(key, 13)
    order = jax.random.permutation(key, GROUPS)
    return (order % 2).astype(jnp.int32)


def draw_cotangent(key, part):
    key = jax.random.fold_in(key, 14)
    key_noise, key_sign, key_chan = jax.random.split(key, 3)
    span = 4 * TAPS
    count = TOKENS // span + 1
    signs = (2 * jax.random.randint(key_sign, (count,), 0, 2) - 1).astype(jnp.float32)
    block_sign = signs[jnp.arange(TOKENS) // span][:, None]
    chan_pos = jnp.arange(D, dtype=jnp.float32)[None, :] / D
    chan_weight = 0.03 * jnp.exp(chan_pos * math.log(10.0)) * (1.0 + jax.random.uniform(key_chan, (1, D), jnp.float32))
    noise = jax.random.truncated_normal(key_noise, -4.0, 4.0, (TOKENS, D), jnp.float32)
    return (noise + block_sign * chan_weight).astype(jnp.bfloat16)


def block_levels(rng, dims, shards, least, largest):
    gain, own = 1.0, jax.random.fold_in(rng, 6)
    for dim, blocks in shards:
        steps = jnp.exp(jax.random.uniform(jax.random.fold_in(own, dim), (blocks,), jnp.float32, least / len(shards), largest / len(shards)))
        gain = gain * jnp.repeat(steps, dims[dim] // blocks).reshape([-1 if axis == dim else 1 for axis in range(len(dims))])
    return gain


def setup_inputs(seed: int = 0) -> dict:
    key_list = jax.random.split(jax.random.key(seed), 8)
    activations = draw_activations(jax.random.fold_in(key_list[7], 71), 0)
    norm_gain = jnp.clip(1.0 + 0.15 * jax.random.normal(key_list[1], (D,), jnp.float32), 0.25, 1.75)
    gate_values = jnp.clip(-0.5 + 2.5 * jax.random.uniform(key_list[2], (TOKENS, D), jnp.float32) ** block_levels(key_list[2], (TOKENS, D), ((0, 128), (1, 2)), -0.2, 0.2), -0.5, 2.0).astype(jnp.bfloat16)
    se_filter = jnp.clip(-0.2 + 1.2 * jax.random.uniform(key_list[3], (SE_TAPS, D), jnp.float32) ** block_levels(key_list[3], (SE_TAPS, D), ((1, 2),), -0.2, 0.2), -0.2, 1.0)
    mr_filter = draw_mr_filter(jax.random.fold_in(key_list[7], 71), 0)
    band_offsets = draw_band_offsets(jax.random.fold_in(key_list[7], 71), 0)
    cotangent = draw_cotangent(jax.random.fold_in(key_list[7], 71), 0)
    return {"activations": activations, "norm_gain": norm_gain, "gate_values": gate_values, "se_filter": se_filter, "mr_filter": mr_filter, "band_offsets": band_offsets, "cotangent": cotangent}


def channel_blocks(array, width):
    length = array.shape[0]
    return array.reshape(length, -1, width).transpose(1, 0, 2)

def unblock(blocks):
    count, length, width = blocks.shape
    return blocks.transpose(1, 0, 2).reshape(length, count * width)

def spectral(triple):
    short_blk, kern_blk, grad_blk = triple
    fft_size = 2 * TOKENS
    spec_short = jnp.fft.rfft(short_blk, fft_size, axis=0)
    spec_kern = jnp.fft.rfft(kern_blk, fft_size, axis=0)
    spec_grad = jnp.fft.rfft(grad_blk, fft_size, axis=0)
    mixed_out = jnp.fft.irfft(spec_short * spec_kern, fft_size, axis=0)[:TOKENS]
    back_grad = jnp.fft.irfft(spec_grad * jnp.conj(spec_kern), fft_size, axis=0)[:TOKENS]
    kern_grad = jnp.fft.irfft(spec_grad * jnp.conj(spec_short), fft_size, axis=0)[:2 * TAPS]
    return (mixed_out.astype(short_blk.dtype), back_grad.astype(short_blk.dtype), kern_grad.astype(short_blk.dtype))

def reference(activations, norm_gain, gate_values, se_filter, mr_filter, band_offsets, cotangent):
    edge_count = SE_TAPS - 1
    act_float = activations.astype(jnp.float32)
    inv_rms = lax.rsqrt(lax.optimization_barrier(jnp.sum(act_float * act_float, axis=1, keepdims=True)) / D + 1e-06)
    normed = act_float * inv_rms
    features = (normed * norm_gain[None, :]).astype(jnp.bfloat16)
    feat_float = features.astype(jnp.float32)
    padded = jnp.pad(feat_float, ((edge_count, 0), (0, 0)))
    short_float = jnp.zeros((TOKENS, D), jnp.float32)
    for tap_index in range(SE_TAPS):
        short_float = short_float + se_filter[tap_index][None, :] * padded[edge_count - tap_index:edge_count - tap_index + TOKENS]
    short_out = short_float.astype(jnp.bfloat16)
    offsets = (band_offsets[:, None] + jnp.zeros((1, GROUP), jnp.int32)).reshape(D)
    upper_flag = offsets[None, :] == 1
    filt = mr_filter.astype(jnp.float32)
    blank_rows = jnp.zeros((TAPS, D), jnp.float32)
    kernel = jnp.where(upper_flag, jnp.concatenate([blank_rows, filt], axis=0), jnp.concatenate([filt, blank_rows], axis=0))
    gate_float = gate_values.astype(jnp.float32)
    grad_out = cotangent.astype(jnp.float32)
    grad_mix = (grad_out * gate_float).astype(jnp.bfloat16)
    width = math.gcd(D, 256)
    mixed_b, back_b, kgrad_b = lax.map(spectral, (channel_blocks(short_out.astype(jnp.float32), width), channel_blocks(kernel, width), channel_blocks(grad_mix.astype(jnp.float32), width)))
    mixed_out = unblock(mixed_b)
    back_grad = unblock(back_b)
    kern_grad = unblock(kgrad_b)
    norm_scale = 1.0 / math.sqrt(TOKENS)
    output = (gate_float * mixed_out).astype(jnp.bfloat16)
    mr_grad = (jnp.where(upper_flag, kern_grad[TAPS:], kern_grad[:TAPS]) * norm_scale).astype(jnp.bfloat16)
    se_rows = []
    for tap_index in range(SE_TAPS):
        se_rows.append(lax.optimization_barrier(jnp.sum(back_grad * padded[edge_count - tap_index:edge_count - tap_index + TOKENS], axis=0)))
    se_grad = jnp.stack(se_rows, axis=0) * norm_scale
    back_pad = jnp.pad(back_grad, ((0, edge_count), (0, 0)))
    feat_grad = jnp.zeros((TOKENS, D), jnp.float32)
    for tap_index in range(SE_TAPS):
        feat_grad = feat_grad + se_filter[tap_index][None, :] * back_pad[tap_index:tap_index + TOKENS]
    gain_grad = lax.optimization_barrier(jnp.sum(feat_grad * normed, axis=0)) * norm_scale
    scaled = feat_grad * norm_gain[None, :]
    inner_sum = lax.optimization_barrier(jnp.sum(scaled * normed, axis=1, keepdims=True))
    input_grad = (inv_rms * (scaled - normed * inner_sum / D)).astype(jnp.bfloat16)
    return (output, input_grad, gain_grad, se_grad, mr_grad)
```

```python
import functools
import math

import jax
import jax.numpy as jnp
import numpy as np
from jax import lax
from jax.experimental import pallas as pl
from jax.experimental.pallas import tpu as pltpu
from jax.sharding import PartitionSpec as P

MESH = pl.DeviceIdType.MESH
CH = 256
BLK = 128
F32 = jnp.float32
BF16 = jnp.bfloat16


def transforms():
    angle = np.pi * (2 * np.arange(BLK)[:, None] + 1) * np.arange(2 * BLK)[None, :] / (2 * BLK)
    forward = np.concatenate([np.cos(angle), -np.sin(angle)], axis=0)
    inverse = forward.T / BLK
    return (
        jnp.asarray(forward, BF16),
        jnp.asarray(inverse[BLK:], BF16),
        jnp.asarray(inverse[:BLK], BF16),
    )


def dot(a, b):
    return jnp.dot(a, b, preferred_element_type=F32)


def remote(src, dst, send_sem, recv_sem, device):
    return pltpu.make_async_remote_copy(
        src_ref=src, dst_ref=dst, send_sem=send_sem, recv_sem=recv_sem,
        device_id=device, device_id_type=MESH,
    )


def both(x):
    return jnp.concatenate([x, x], axis=1)


def fold(x):
    return jnp.sum(x.reshape(x.shape[0] // 8, 8, x.shape[1]), axis=0)


def kernel(
    pn, zn, seq_size, dim, scale,
    act_h, gain_ref, gate_h, se_ref, mrf_h, off_ref, cot_h, fwd_ref, inv_hi_ref, inv_lo_ref,
    out_h, ig_h, gg_ref, seg_ref, mr_h,
    act, gate, cot, mrf, g_own, g_halo, s_own, s_halo, f_ext, tail_in, b_ext, head_in, spec,
    out_v, ig_v, row_acc, row_out, row_in, inv_rms, row2_out, row2_in,
    red, core_in, xy_out, xys_out, xy_in, xys_in, own_sum, z_out, z_in, mr_all, sg_all,
    in_sem, out_sem, g_send, g_recv, s_send, s_recv, edge_send, edge_recv, row_send, row_recv,
    core_send, core_recv, xy_send, xy_recv, xys_send, xys_recv, z_send, z_recv,
    zg_send, zg_recv, xg_send, xg_recv, xgs_send, xgs_recv, cg_send, cg_recv,
):
    nc = act.shape[0]
    rows = act.shape[1]
    seq = lax.axis_index("seq")
    tp = lax.axis_index("tp")
    core = lax.rem(seq, 2)
    z = lax.rem(seq // 2, zn)
    xy = seq // (2 * zn)
    after = (lax.rem(seq + 1, seq_size), tp)
    before = (lax.rem(seq + seq_size - 1, seq_size), tp)
    pair = (seq, 1 - tp)
    other_core = (seq + 1 - 2 * core, tp)

    def xy_peer(p):
        return (p * (2 * zn) + z * 2 + core, tp)

    def z_peer(j):
        return (xy * (2 * zn) + j * 2 + core, tp)

    def lanes(c):
        return pl.ds(pl.multiple_of(c * CH, CH), CH)

    def in_copy(n, c):
        src, dst = ((act_h, act), (gate_h, gate), (cot_h, cot), (mrf_h, mrf))[n]
        return pltpu.make_async_copy(src.at[:, lanes(c)], dst.at[c], in_sem.at[n, c])

    def loop(body, count=nc):
        def step(c, carry):
            body(c)
            return carry

        lax.fori_loop(0, count, step, 0)

    for n in range(4):
        loop(lambda c, n=n: in_copy(n, c).start())

    barrier = pltpu.get_barrier_semaphore()
    partners = [after, before, pair, other_core]
    partners += [xy_peer(lax.rem(xy + d, pn)) for d in range(1, pn)]
    partners += [z_peer(lax.rem(z + d, zn)) for d in range(1, zn)]
    for partner in partners:
        pl.semaphore_signal(barrier, inc=1, device_id=partner, device_id_type=MESH)
    pl.semaphore_wait(barrier, len(partners))

    row_acc[...] = jnp.zeros_like(row_acc)

    def squares(c):
        in_copy(0, c).wait()
        a = act[c].astype(F32)
        a = a * a
        row_acc[...] += a[:, :BLK] + a[:, BLK:]

    loop(squares)
    row_out[...] = jnp.broadcast_to(jnp.sum(row_acc[...], axis=1, keepdims=True), row_out.shape)
    row_copy = remote(row_out, row_in, row_send.at[0], row_recv.at[0], pair)
    row_copy.start()

    def g_copy(c):
        return remote(g_own.at[c], g_halo.at[c], g_send.at[c], g_recv.at[c], before)

    def gated(c):
        in_copy(1, c).wait()
        in_copy(2, c).wait()
        g_own[c] = (cot[c].astype(F32) * gate[c].astype(F32)).astype(BF16)
        g_copy(c).start()

    loop(gated)

    row_copy.wait()
    inv_rms[...] = lax.rsqrt((row_out[...] + row_in[...]) / dim + 1e-06)

    def featured(c):
        inv = both(inv_rms[...])
        f = (act[c].astype(F32) * inv * gain_ref[:, lanes(c)]).astype(BF16)
        f_ext[c, 8:, :] = f.astype(F32)

    loop(featured)
    tail_copy = remote(
        f_ext.at[:, pl.ds(rows, 8), :], tail_in, edge_send.at[0], edge_recv.at[0], after
    )
    tail_copy.start()

    def filtered(c):
        in_copy(3, c).wait()
        spec[c] = dot(fwd_ref[:, :BLK], mrf[c])

    loop(filtered)

    tail_copy.wait()

    @pl.when(seq == 0)
    def _():
        tail_in[...] = jnp.zeros_like(tail_in)

    def s_copy(c):
        return remote(s_own.at[c], s_halo.at[c], s_send.at[c], s_recv.at[c], after)

    def short(c):
        f_ext[c, :8, :] = tail_in[c]
        taps = se_ref[:, lanes(c)]
        for r in range(0, rows, 64):
            total = taps[0:1] * f_ext[c, 8 + r : 72 + r, :]
            for k in range(1, 7):
                total = total + taps[k : k + 1] * f_ext[c, 8 + r - k : 72 + r - k, :]
            s_own[c, r : r + 64, :] = total.astype(BF16)
        s_copy(c).start()

    loop(short)

    def upper(c):
        left = jnp.full((BLK, BLK), off_ref[2 * c], jnp.int32)
        right = jnp.full((BLK, BLK), off_ref[2 * c + 1], jnp.int32)
        return jnp.concatenate([left, right], axis=1).astype(F32).astype(BF16) > 0.5

    def backward(c):
        g_copy(c).wait()

        @pl.when(seq == seq_size - 1)
        def _():
            g_halo[c] = jnp.zeros_like(g_halo[c])

        up = upper(c)
        g0, g1 = g_own[c, :BLK], g_own[c, BLK:]
        g2, g3 = g_halo[c, :BLK], g_halo[c, BLK:]
        v0, v1, v2 = jnp.where(up, g1, g0), jnp.where(up, g2, g1), jnp.where(up, g3, g2)
        hr, hi = spec[c, :BLK], spec[c, BLK:]
        for n, window in enumerate(((v0, v1), (v1, v2))):
            v = dot(fwd_ref[...], jnp.concatenate(window, axis=0))
            vr, vi = v[:BLK], v[BLK:]
            prod = jnp.concatenate([hr * vr + hi * vi, hr * vi - hi * vr], axis=0).astype(BF16)
            b_ext[c, n * BLK : (n + 1) * BLK, :] = dot(inv_lo_ref[...], prod)

    loop(backward)
    head_copy = remote(
        b_ext.at[:, pl.ds(0, 8), :], head_in, edge_send.at[1], edge_recv.at[1], before
    )
    head_copy.start()

    def out_copy(c):
        return pltpu.make_async_copy(out_v.at[c], out_h.at[:, lanes(c)], out_sem.at[0, c])

    def forward(c):
        s_copy(c).wait()

        @pl.when(seq == 0)
        def _():
            s_halo[c] = jnp.zeros_like(s_halo[c])

        up = upper(c)
        s0, s1 = s_halo[c, :BLK], s_halo[c, BLK:]
        s2, s3 = s_own[c, :BLK], s_own[c, BLK:]
        w0, w1, w2 = jnp.where(up, s0, s1), jnp.where(up, s1, s2), jnp.where(up, s2, s3)
        hr, hi = spec[c, :BLK], spec[c, BLK:]
        kr, ki = 0.0, 0.0
        for n, window in enumerate(((w0, w1), (w1, w2))):
            at = slice(n * BLK, (n + 1) * BLK)
            w = dot(fwd_ref[...], jnp.concatenate(window, axis=0))
            wr, wi = w[:BLK], w[BLK:]
            q = dot(fwd_ref[:, BLK:], g_own[c, at])
            qr, qi = q[:BLK], q[BLK:]
            kr = kr + (wr * qr + wi * qi)
            ki = ki + (wr * qi - wi * qr)
            prod = jnp.concatenate([hr * wr - hi * wi, hr * wi + hi * wr], axis=0).astype(BF16)
            y = dot(inv_hi_ref[...], prod)
            out_v[c, at] = (gate[c, at].astype(F32) * y).astype(BF16)
        kk = jnp.concatenate([kr, ki], axis=0)
        top = kk.astype(BF16)
        low = (kk - top.astype(F32)).astype(BF16)
        red[c, :BLK, :] = dot(inv_lo_ref[...], top) + dot(inv_lo_ref[...], low)
        out_copy(c).start()

    loop(forward)

    head_copy.wait()

    @pl.when(seq == seq_size - 1)
    def _():
        head_in[...] = jnp.zeros_like(head_in)

    row_acc[...] = jnp.zeros_like(row_acc)

    def back_short(c):
        b_ext[c, rows:, :] = head_in[c]
        taps = se_ref[:, lanes(c)]
        gain = gain_ref[:, lanes(c)]
        sums = [jnp.zeros((8, CH), F32)] * 8
        for r in range(0, rows, 64):
            at = slice(r, r + 64)
            b = b_ext[c, at, :]
            grad = taps[0:1] * b
            for k in range(1, 7):
                grad = grad + taps[k : k + 1] * b_ext[c, r + k : r + k + 64, :]
            for k in range(7):
                sums[k] = sums[k] + fold(b * f_ext[c, 8 + r - k : 72 + r - k, :])
            normed = act[c, at].astype(F32) * both(inv_rms[at])
            sums[7] = sums[7] + fold(grad * normed)
            scaled = grad * gain
            inner = scaled * normed
            row_acc[at] += inner[:, :BLK] + inner[:, BLK:]
            spec[c, at, :] = scaled
        for k in range(8):
            red[c, BLK + k : BLK + k + 1, :] = jnp.sum(sums[k], axis=0, keepdims=True)

    loop(back_short)
    row2_out[...] = jnp.broadcast_to(jnp.sum(row_acc[...], axis=1, keepdims=True), row2_out.shape)
    row2_copy = remote(row2_out, row2_in, row_send.at[1], row_recv.at[1], pair)
    row2_copy.start()

    core_copy = remote(
        red.at[pl.ds((1 - core) * pn, pn)], core_in, core_send.at[0], core_recv.at[0], other_core
    )
    core_copy.start()

    row2_copy.wait()
    row2_in[...] = (row2_out[...] + row2_in[...]) / dim

    def ig_copy(c):
        return pltpu.make_async_copy(ig_v.at[c], ig_h.at[:, lanes(c)], out_sem.at[1, c])

    def finish(c):
        inv = both(inv_rms[...])
        normed = act[c].astype(F32) * inv
        ig_v[c] = (inv * (spec[c] - normed * both(row2_in[...]))).astype(BF16)
        ig_copy(c).start()

    loop(finish)

    core_copy.wait()

    def xy_copy(p):
        return remote(xy_out.at[p], xy_in.at[xy], xy_send.at[p], xy_recv.at[xy], xy_peer(p))

    def xys_copy(p):
        return remote(xys_out.at[p], xys_in.at[xy], xys_send.at[p], xys_recv.at[xy], xy_peer(p))

    for d in range(1, pn):
        p = lax.rem(xy + d, pn)
        q = red[core * pn + p] + core_in[p]
        xy_out[p] = q[:BLK].astype(BF16)
        xys_out[p] = q[BLK:]
        xy_copy(p).start()
        xys_copy(p).start()
    own_sum[...] = red[core * pn + xy] + core_in[xy]
    for d in range(1, pn):
        p = lax.rem(xy + d, pn)
        xy_copy(p).wait_send()
        xys_copy(p).wait_send()
        remote(xy_out.at[p], xy_in.at[p], xy_send.at[p], xy_recv.at[p], xy_peer(p)).wait_recv()
        remote(xys_out.at[p], xys_in.at[p], xys_send.at[p], xys_recv.at[p], xy_peer(p)).wait_recv()
        own_sum[:BLK, :] += xy_in[p].astype(F32)
        own_sum[BLK:, :] += xys_in[p]

    part = BLK // zn
    for j in range(zn):
        z_out[j, :part, :] = own_sum[j * part : (j + 1) * part, :]
        z_out[j, part:, :] = own_sum[BLK:, :]

    def z_copy(j):
        return remote(z_out.at[j], z_in.at[z], z_send.at[j], z_recv.at[z], z_peer(j))

    for d in range(1, zn):
        z_copy(lax.rem(z + d, zn)).start()
    z_in[z] = z_out[z]
    for d in range(1, zn):
        j = lax.rem(z + d, zn)
        z_copy(j).wait_send()
        remote(z_out.at[j], z_in.at[j], z_send.at[j], z_recv.at[j], z_peer(j)).wait_recv()
    total = z_in[0]
    for j in range(1, zn):
        total = total + z_in[j]
    total = total * scale

    mine = core * pn + xy
    mr_all[mine, pl.ds(pl.multiple_of(z * part, part), part), :] = total[:part].astype(BF16)
    sg_all[mine] = total[part:]

    def piece(j):
        return mr_all.at[mine, pl.ds(pl.multiple_of(j * part, part), part), :]

    for d in range(1, zn):
        j = lax.rem(z + d, zn)
        remote(piece(z), piece(z), zg_send.at[j], zg_recv.at[z], z_peer(j)).start()
    for d in range(1, zn):
        j = lax.rem(z + d, zn)
        remote(piece(z), piece(z), zg_send.at[j], zg_recv.at[z], z_peer(j)).wait_send()
        remote(piece(j), piece(j), zg_send.at[j], zg_recv.at[j], z_peer(j)).wait_recv()

    for d in range(1, pn):
        p = lax.rem(xy + d, pn)
        remote(mr_all.at[mine], mr_all.at[mine], xg_send.at[p], xg_recv.at[xy], xy_peer(p)).start()
        remote(sg_all.at[mine], sg_all.at[mine], xgs_send.at[p], xgs_recv.at[xy], xy_peer(p)).start()
    for d in range(1, pn):
        p = lax.rem(xy + d, pn)
        theirs = core * pn + p
        remote(mr_all.at[mine], mr_all.at[mine], xg_send.at[p], xg_recv.at[xy], xy_peer(p)).wait_send()
        remote(sg_all.at[mine], sg_all.at[mine], xgs_send.at[p], xgs_recv.at[xy], xy_peer(p)).wait_send()
        remote(mr_all.at[theirs], mr_all.at[theirs], xg_send.at[p], xg_recv.at[p], xy_peer(p)).wait_recv()
        remote(sg_all.at[theirs], sg_all.at[theirs], xgs_send.at[p], xgs_recv.at[p], xy_peer(p)).wait_recv()

    def halves(n, ref, k):
        half = ref.at[pl.ds(k * pn, pn)]
        return remote(half, half, cg_send.at[n], cg_recv.at[n], other_core)

    for n, ref in enumerate((mr_all, sg_all)):
        halves(n, ref, core).start()
    for n, ref in enumerate((mr_all, sg_all)):
        halves(n, ref, core).wait_send()
        halves(n, ref, 1 - core).wait_recv()

    def mr_copy(c):
        return pltpu.make_async_copy(mr_all.at[c], mr_h.at[:, lanes(c)], out_sem.at[2, c])

    def spread(c):
        mr_copy(c).start()
        seg_ref[:, lanes(c)] = sg_all[c, :7, :]
        gg_ref[:, lanes(c)] = sg_all[c, 7:8, :]

    loop(spread)

    def drain(c):
        out_copy(c).wait()
        ig_copy(c).wait()
        mr_copy(c).wait()

    loop(drain)


def per_device(seq_size, dim, tokens, act, gain, gate, se, mrf, off, cot):
    rows, chans = act.shape
    nc = chans // CH
    zn = 8 if seq_size == 128 else 2
    pn = seq_size // (2 * zn)
    assert nc == 2 * pn and rows == 2 * BLK and mrf.shape[0] == BLK and se.shape[0] == 7
    fwd, inv_hi, inv_lo = transforms()
    any_spec = pl.BlockSpec(memory_space=pl.ANY)
    vmem = pl.BlockSpec(memory_space=pltpu.VMEM)
    smem = pl.BlockSpec(memory_space=pltpu.SMEM)
    dma = pltpu.SemaphoreType.DMA
    part = BLK // zn
    V = pltpu.VMEM
    scratch = [
        V((nc, rows, CH), BF16), V((nc, rows, CH), BF16), V((nc, rows, CH), BF16), V((nc, BLK, CH), BF16),
        V((nc, rows, CH), BF16), V((nc, rows, CH), BF16), V((nc, rows, CH), BF16), V((nc, rows, CH), BF16),
        V((nc, rows + 8, CH), F32), V((nc, 8, CH), F32), V((nc, rows + 8, CH), F32), V((nc, 8, CH), F32),
        V((nc, rows, CH), F32),
        V((nc, rows, CH), BF16), V((nc, rows, CH), BF16),
        V((rows, BLK), F32), V((rows, BLK), F32), V((rows, BLK), F32), V((rows, BLK), F32),
        V((rows, BLK), F32), V((rows, BLK), F32),
        V((nc, BLK + 8, CH), F32), V((pn, BLK + 8, CH), F32),
        V((pn, BLK, CH), BF16), V((pn, 8, CH), F32), V((pn, BLK, CH), BF16), V((pn, 8, CH), F32),
        V((BLK + 8, CH), F32), V((zn, part + 8, CH), F32), V((zn, part + 8, CH), F32),
        V((nc, BLK, CH), BF16), V((nc, 8, CH), F32),
        dma((4, nc)), dma((3, nc)), dma((nc,)), dma((nc,)), dma((nc,)), dma((nc,)),
        dma((2,)), dma((2,)), dma((2,)), dma((2,)),
        dma((1,)), dma((1,)), dma((pn,)), dma((pn,)), dma((pn,)), dma((pn,)),
        dma((zn,)), dma((zn,)), dma((zn,)), dma((zn,)),
        dma((pn,)), dma((pn,)), dma((pn,)), dma((pn,)), dma((2,)), dma((2,)),
    ]
    out, ig, gg, seg, mr = pl.pallas_call(
        functools.partial(kernel, pn, zn, seq_size, dim, 1.0 / math.sqrt(tokens)),
        out_shape=(
            jax.ShapeDtypeStruct((rows, chans), BF16),
            jax.ShapeDtypeStruct((rows, chans), BF16),
            jax.ShapeDtypeStruct((1, chans), F32),
            jax.ShapeDtypeStruct((7, chans), F32),
            jax.ShapeDtypeStruct((BLK, chans), BF16),
        ),
        in_specs=[any_spec, vmem, any_spec, vmem, any_spec, smem, any_spec, vmem, vmem, vmem],
        out_specs=(any_spec, any_spec, vmem, vmem, any_spec),
        scratch_shapes=scratch,
        compiler_params=pltpu.CompilerParams(
            collective_id=0, has_side_effects=True, vmem_limit_bytes=58 * 1024 * 1024
        ),
        name="hyena",
    )(act, gain.reshape(1, chans), gate, se, mrf, off, cot, fwd, inv_hi, inv_lo)
    return out, ig, gg.reshape(chans), seg, mr


def solution(mesh):
    in_specs = (
        P("seq", "tp"), P("tp"), P("seq", "tp"), P(None, "tp"), P(None, "tp"), P("tp"), P("seq", "tp"),
    )
    out_specs = (P("seq", "tp"), P("seq", "tp"), P("tp"), P(None, "tp"), P(None, "tp"))

    def whole(act, *rest):
        tokens, dim = act.shape
        body = functools.partial(per_device, mesh.shape["seq"], dim, tokens)
        return jax.shard_map(
            body, mesh=mesh, in_specs=in_specs, out_specs=out_specs, check_vma=False
        )(act, *rest)

    return whole
```

```python
import functools
import math

import jax
import jax.numpy as jnp
import numpy as np
from jax import lax
from jax.experimental import pallas as pl
from jax.experimental.pallas import tpu as pltpu
from jax.sharding import PartitionSpec as P

MESH = pl.DeviceIdType.MESH
CH = 256
BLK = 128
SE = 7
LAGS = BLK + 8
LATE = 3
F32 = jnp.float32
BF16 = jnp.bfloat16


def transforms():
    angle = np.pi * (2 * np.arange(BLK)[:, None] + 1) * np.arange(2 * BLK)[None, :] / (2 * BLK)
    forward = np.concatenate([np.cos(angle), -np.sin(angle)], axis=0)
    inverse = forward.T / BLK
    return (
        jnp.asarray(forward, BF16),
        jnp.asarray(inverse[BLK:], BF16),
        jnp.asarray(np.concatenate([inverse[:LAGS], inverse[:LAGS]], axis=1), BF16),
    )


def dot(a, b):
    return jnp.dot(a, b, preferred_element_type=F32)


def remote(src, dst, send_sem, recv_sem, device):
    return pltpu.make_async_remote_copy(
        src_ref=src, dst_ref=dst, send_sem=send_sem, recv_sem=recv_sem,
        device_id=device, device_id_type=MESH,
    )


def both(x):
    return jnp.concatenate([x, x], axis=1)


def split(x):
    top = x.astype(BF16)
    return top, (x - top.astype(F32)).astype(BF16)


def kernel(
    pn, zn, seq_size, dim, scale,
    act_h, gain_ref, gate_h, se_ref, mrf_h, off_ref, cot_h, fwd_ref, inv_hi_ref, inv_lo_ref,
    out_h, ig_h, gg_ref, seg_ref, mr_h,
    act, gate, cot, mrf, g_own, g_halo, s_own, s_halo, zeros, f_own, f_ext, tail_out, tail_in, b_ext, head_in, spec,
    out_v, ig_v, row_acc, row_out, row_in, inv_rms, row2_out, row2_in, no_rows, mean2,
    red, core_in, xy_out, xy_in, own_sum, z_out, z_in, z_last_out, z_last_in, lags, mr_all,
    in_sem, out_sem, g_send, g_recv, s_send, s_recv, tail_send, tail_recv, head_send, head_recv, row_send, row_recv,
    core_send, core_recv, xy_send, xy_recv, z_send, z_recv, zl_send, zl_recv, zg_send, zg_recv, zgl_send, zgl_recv, xg_send, xg_recv, cg_send, cg_recv,
):
    nc = act.shape[0]
    rows = act.shape[1]
    seq = lax.axis_index("seq")
    tp = lax.axis_index("tp")
    core = lax.rem(seq, 2)
    z = lax.rem(seq // 2, zn)
    xy = seq // (2 * zn)
    first = seq == 0
    last = seq == seq_size - 1
    after = (lax.rem(seq + 1, seq_size), tp)
    before = (lax.rem(seq + seq_size - 1, seq_size), tp)
    pair = (seq, 1 - tp)
    other_core = (seq + 1 - 2 * core, tp)

    def xy_peer(p):
        return (p * (2 * zn) + z * 2 + core, tp)

    def z_peer(j):
        return (xy * (2 * zn) + j * 2 + core, tp)

    def turn(start, t):
        return lax.rem(start + pn - t, pn)

    before_xy = lax.rem(seq + seq_size - 1, seq_size) // (2 * zn)

    def lanes(c):
        return pl.ds(pl.multiple_of(c * CH, CH), CH)

    def in_copy(n, c):
        src, dst = ((act_h, act), (gate_h, gate), (cot_h, cot), (mrf_h, mrf))[n]
        return pltpu.make_async_copy(src.at[:, lanes(c)], dst.at[c], in_sem.at[n, c])

    def loop(body, start=0, stop=nc):
        def step(c, carry):
            body(c)
            return carry

        lax.fori_loop(start, stop, step, 0)

    barrier = pltpu.get_barrier_semaphore()
    partners = [after, before, pair, other_core]
    partners += [xy_peer(lax.rem(xy + d, pn)) for d in range(1, pn)]
    partners += [z_peer(lax.rem(z + d, zn)) for d in range(1, zn)]
    for partner in partners:
        pl.semaphore_signal(barrier, inc=1, device_id=partner, device_id_type=MESH)

    def fetch(t):
        i = turn(before_xy, t)
        for c in (2 * i, 2 * i + 1):
            in_copy(1, c).start()
            in_copy(2, c).start()

    pairs = nc // 2
    loop(lambda c: in_copy(0, c).start())
    loop(fetch, 0, pairs)
    loop(lambda c: in_copy(3, c).start())

    zeros[...] = jnp.zeros_like(zeros)
    no_rows[...] = jnp.zeros_like(no_rows)
    row_acc[...] = jnp.zeros_like(row_acc)

    def squares(c):
        in_copy(0, c).wait()
        a = act[c].astype(F32)
        a = a * a
        row_acc[...] += a[:, :BLK] + a[:, BLK:]

    def across(acc):
        return jnp.broadcast_to(jnp.sum(jnp.transpose(acc), axis=0, keepdims=True), (8, rows))

    def down(x):
        return jnp.broadcast_to(jnp.transpose(x)[:, :1], (rows, BLK))

    pl.semaphore_wait(barrier, len(partners))

    loop(squares)
    row_out[...] = across(row_acc[...])
    row_copy = remote(row_out, row_in, row_send.at[0], row_recv.at[0], pair)
    row_copy.start()

    def g_copy(c, src=None):
        return remote(g_own.at[c] if src is None else src, g_halo.at[c], g_send.at[c], g_recv.at[c], before)

    def gated(c):
        in_copy(1, c).wait()
        in_copy(2, c).wait()
        g_own[c] = (cot[c].astype(F32) * gate[c].astype(F32)).astype(BF16)

        @pl.when(first)
        def _():
            g_copy(c, zeros).start()

        @pl.when(jnp.logical_not(first))
        def _():
            g_copy(c).start()

    def gated_pair(t):
        i = turn(before_xy, t)
        for c in (2 * i, 2 * i + 1):
            gated(c)

    loop(gated_pair, 0, pairs)

    def filtered(i):
        for n in range(4):
            in_copy(3, 4 * i + n).wait()
        for n in range(4):
            spec[4 * i + n] = dot(fwd_ref[:, :BLK], mrf[4 * i + n])

    loop(filtered, 0, nc // 4)

    row_copy.wait()
    inv_rms[...] = down(lax.rsqrt((row_out[...] + row_in[...]) / dim + 1e-06))

    def feature(c, at):
        return (act[c, at].astype(F32) * both(inv_rms[at]) * gain_ref[:, lanes(c)]).astype(BF16)

    def tail(c):
        end = feature(c, slice(rows - 16, rows)).astype(F32)
        tail_out[c] = jnp.where(last, 0.0, end[8:])

    loop(tail)
    tail_copy = remote(tail_out, tail_in, tail_send.at[0], tail_recv.at[0], after)
    tail_copy.start()

    def short_rows(c, r, count):
        taps = se_ref[:, lanes(c)]
        total = taps[0:1] * f_ext[c, 8 + r : 8 + r + count, :]
        for k in range(1, SE):
            total = total + taps[k : k + 1] * f_ext[c, 8 + r - k : 8 + r + count - k, :]
        s_own[c, r : r + count, :] = total.astype(BF16)

    def featured(c):
        f = feature(c, slice(0, rows))
        f_own[c] = f
        f_ext[c, 8:, :] = f.astype(F32)
        short_rows(c, 16, 48)
        for r in range(64, rows, 64):
            short_rows(c, r, 64)

    loop(featured)
    tail_copy.wait()

    def s_copy(c, src=None):
        return remote(s_own.at[c] if src is None else src, s_halo.at[c], s_send.at[c], s_recv.at[c], after)

    def short(c):
        f_ext[c, :8, :] = tail_in[c]
        short_rows(c, 0, 16)

        @pl.when(last)
        def _():
            s_copy(c, zeros).start()

        @pl.when(jnp.logical_not(last))
        def _():
            s_copy(c).start()

    loop(short)

    def upper(c):
        left = jnp.full((BLK, BLK), off_ref[2 * c], jnp.int32)
        right = jnp.full((BLK, BLK), off_ref[2 * c + 1], jnp.int32)
        return jnp.concatenate([left, right], axis=1).astype(F32)

    def backward(c):
        flag = upper(c)
        up = flag.astype(BF16) > 0.5
        g0, g1 = g_own[c, :BLK], g_own[c, BLK:]
        g2, g3 = g_halo[c, :BLK], g_halo[c, BLK:]
        v0, v1, v2 = jnp.where(up, g1, g0), jnp.where(up, g2, g1), jnp.where(up, g3, g2)
        hr, hi = spec[c, :BLK], spec[c, BLK:]
        kr, ki = 0.0, 0.0
        for n, window in enumerate(((v0, v1), (v1, v2))):
            at = slice(n * BLK, (n + 1) * BLK)
            v = dot(fwd_ref[...], jnp.concatenate(window, axis=0))
            vr, vi = v[:BLK], v[BLK:]
            prod = jnp.concatenate([hr * vr + hi * vi, hr * vi - hi * vr], axis=0).astype(BF16)
            b_ext[c, at, :] = dot(inv_lo_ref[:BLK, : 2 * BLK], prod)
            s = dot(fwd_ref[:, :BLK], f_own[c, at])
            sr, si = s[:BLK], s[BLK:]
            kr = kr + (sr * vr + si * vi)
            ki = ki + (sr * vi - si * vr)
        top, low = split(jnp.concatenate([kr, ki], axis=0))
        x = dot(inv_lo_ref[...], jnp.concatenate([top, low], axis=0))
        red[c, :BLK, :] = x[:BLK]
        up8 = flag[:8] > 0.5
        f0 = f_own[c, BLK - 16 : BLK].astype(F32)[8:]
        f1 = f_own[c, rows - 16 : rows].astype(F32)[8:]
        fa, fb = jnp.where(up8, tail_in[c], f0), jnp.where(up8, f0, f1)
        ua = g0[:16].astype(F32)[:8] + g2[:16].astype(F32)[:8]
        ub = g1[:16].astype(F32)[:8] + g3[:16].astype(F32)[:8]
        row = lax.broadcasted_iota(jnp.int32, (8, CH), 0)
        fix = x[BLK:]
        for r in range(1, SE - 1):
            term = pltpu.roll(fa, r, 0) * ua + pltpu.roll(fb, r, 0) * ub
            term = jnp.sum(jnp.where(row < r, term, 0.0), axis=0, keepdims=True)
            fix = fix + jnp.where(row == r, term, 0.0)
        red[c, BLK:, :] = fix

    def head_copy(c, src=None):
        src = b_ext.at[c, pl.ds(0, 8), :] if src is None else src
        return remote(src, head_in.at[c], head_send.at[c], head_recv.at[c], before)

    def core_copy(i):
        return remote(red.at[2 * i + 1 - core], core_in.at[i], core_send.at[i], core_recv.at[i], other_core)

    def backward_pair(t):
        i = turn(xy, t)
        for c in (2 * i, 2 * i + 1):
            g_copy(c).wait_recv()
        for c in (2 * i, 2 * i + 1):
            backward(c)
        core_copy(i).start()
        for c in (2 * i, 2 * i + 1):

            @pl.when(first)
            def _(c=c):
                head_copy(c, no_rows).start()

            @pl.when(jnp.logical_not(first))
            def _(c=c):
                head_copy(c).start()

    def back_short(c):
        b_ext[c, rows:, :] = head_in[c]
        taps = se_ref[:, lanes(c)]
        gain = gain_ref[:, lanes(c)]
        for r in range(0, rows, 64):
            at = slice(r, r + 64)
            grad = taps[0:1] * b_ext[c, at, :]
            for k in range(1, SE):
                grad = grad + taps[k : k + 1] * b_ext[c, r + k : r + k + 64, :]
            scaled = grad * gain
            inner = scaled * (act[c, at].astype(F32) * both(inv_rms[at]))
            row_acc[at] += inner[:, :BLK] + inner[:, BLK:]
            f_ext[c, at, :] = scaled

    def back_short_pair(t):
        i = turn(xy, t)
        for c in (2 * i, 2 * i + 1):
            head_copy(c).wait_recv()
        for c in (2 * i, 2 * i + 1):
            back_short(c)

    def xy_copy(p):
        return remote(xy_out.at[p], xy_in.at[xy], xy_send.at[p], xy_recv.at[xy], xy_peer(p))

    def xy_start(t):
        i = turn(xy, t)
        core_copy(i).wait()
        q = red[2 * i + core] + core_in[i]

        @pl.when(i == xy)
        def _():
            own_sum[...] = q

        @pl.when(i != xy)
        def _():
            xy_out[i, :BLK, :] = q[:BLK].astype(BF16)
            top = q[BLK:].astype(BF16).astype(F32)
            xy_out[i, BLK:, :] = jnp.concatenate([top, q[BLK:] - top], axis=0).astype(BF16)
            xy_copy(i).start()

    def out_copy(c):
        return pltpu.make_async_copy(out_v.at[c], out_h.at[:, lanes(c)], out_sem.at[0, c])

    def forward(c):
        up = upper(c).astype(BF16) > 0.5
        s0, s1 = s_halo[c, :BLK], s_halo[c, BLK:]
        s2, s3 = s_own[c, :BLK], s_own[c, BLK:]
        w0, w1, w2 = jnp.where(up, s0, s1), jnp.where(up, s1, s2), jnp.where(up, s2, s3)
        hr, hi = spec[c, :BLK], spec[c, BLK:]
        for n, window in enumerate(((w0, w1), (w1, w2))):
            at = slice(n * BLK, (n + 1) * BLK)
            w = dot(fwd_ref[...], jnp.concatenate(window, axis=0))
            wr, wi = w[:BLK], w[BLK:]
            prod = jnp.concatenate([hr * wr - hi * wi, hr * wi + hi * wr], axis=0).astype(BF16)
            y = dot(inv_hi_ref[...], prod)
            out_v[c, at] = (gate[c, at].astype(F32) * y).astype(BF16)

    def forward_pair(i):
        for c in (2 * i, 2 * i + 1):
            s_copy(c).wait()
        for c in (2 * i, 2 * i + 1):
            forward(c)
        for c in (2 * i, 2 * i + 1):
            out_copy(c).start()

    part = BLK // zn
    end = zn - 1

    def z_copy(j):
        return remote(z_out.at[j], z_in.at[z], z_send.at[j], z_recv.at[z], z_peer(j))

    def z_last_copy():
        return remote(z_last_out, z_last_in.at[z], zl_send.at[0], zl_recv.at[z], z_peer(end))

    def z_start():
        for d in range(1, pn):
            p = lax.rem(xy + d, pn)
            remote(xy_out.at[p], xy_in.at[p], xy_send.at[p], xy_recv.at[p], xy_peer(p)).wait_recv()
        total = own_sum[...]
        for d in range(1, pn):
            x = xy_in[lax.rem(xy + d, pn)].astype(F32)
            total = total + jnp.concatenate([x[:BLK], x[BLK : BLK + 8] + x[BLK + 8 :]], axis=0)
        for j in range(zn):
            z_out[j] = total[j * part : (j + 1) * part]
        z_last_out[...] = total[BLK:]
        for d in range(1, zn):
            z_copy(lax.rem(z + d, zn)).start()

        @pl.when(z != end)
        def _():
            z_last_copy().start()

    def piece(j):
        return lags.at[pl.ds(pl.multiple_of(j * part, part), part), :]

    def zg_copy(i, j):
        return remote(piece(i), piece(i), zg_send.at[j], zg_recv.at[i], z_peer(j))

    def zg_last_copy(j):
        rest = lags.at[pl.ds(BLK, 8), :]
        return remote(rest, rest, zgl_send.at[j], zgl_recv.at[0], z_peer(j))

    def z_sum():
        total = z_out[z]
        for d in range(1, zn):
            j = lax.rem(z + d, zn)
            remote(z_out.at[j], z_in.at[j], z_send.at[j], z_recv.at[j], z_peer(j)).wait_recv()
            total = total + z_in[j]
        lags[pl.ds(pl.multiple_of(z * part, part), part), :] = total
        for d in range(1, zn):
            zg_copy(z, lax.rem(z + d, zn)).start()

        @pl.when(z == end)
        def _():
            rest = z_last_out[...]
            for j in range(zn - 1):
                remote(z_last_out, z_last_in.at[j], zl_send.at[0], zl_recv.at[j], z_peer(j)).wait_recv()
                rest = rest + z_last_in[j]
            lags[BLK:, :] = rest
            for j in range(zn - 1):
                zg_last_copy(j).start()

    def xg_copy(p, q):
        half = mr_all.at[p, core]
        return remote(half, half, xg_send.at[q], xg_recv.at[p], xy_peer(q))

    def grads_start():
        for d in range(1, zn):
            j = lax.rem(z + d, zn)
            zg_copy(z, j).wait_send()
            zg_copy(j, j).wait_recv()

        @pl.when(z != end)
        def _():
            z_last_copy().wait_send()
            zg_last_copy(end).wait_recv()

        @pl.when(z == end)
        def _():
            for j in range(zn - 1):
                zg_last_copy(j).wait_send()

        mine = 2 * xy + core
        taps = se_ref[:, lanes(mine)]
        filt = mrf[mine].astype(F32)
        grads = []
        kern = jnp.zeros((BLK, CH), F32)
        gain_sum = jnp.zeros((1, CH), F32)
        for k in range(SE):
            x = lags[k : k + BLK, :]
            kern = kern + taps[k : k + 1] * x
            grads.append(jnp.sum(filt * x, axis=0, keepdims=True) * scale)
            gain_sum = gain_sum + taps[k : k + 1] * grads[k]
        grads.append(gain_sum / gain_ref[:, lanes(mine)])
        grads = jnp.concatenate(grads, axis=0)
        top = grads.astype(BF16).astype(F32)
        mr_all[xy, core, :BLK, :] = (kern * scale).astype(BF16)
        mr_all[xy, core, BLK:, :] = jnp.concatenate([top, grads - top], axis=0).astype(BF16)
        for d in range(1, pn):
            xg_copy(xy, lax.rem(xy + d, pn)).start()

    row_acc[...] = jnp.zeros_like(row_acc)
    backward_pair(0)

    def early(t):
        backward_pair(t)
        xy_start(t - 1)

    loop(early, 1, min(LATE, pairs))

    def middle(t):
        backward_pair(t)
        back_short_pair(t - LATE)
        xy_start(t - 1)

    loop(middle, LATE, pairs)
    xy_start(pairs - 1)
    loop(back_short_pair, max(pairs - LATE, 0), pairs)
    row2_out[...] = across(row_acc[...])
    row2_copy = remote(row2_out, row2_in, row_send.at[1], row_recv.at[1], pair)
    row2_copy.start()

    quarter = max(pairs // 4, 1)
    loop(forward_pair, 0, quarter)
    z_start()
    loop(forward_pair, quarter, min(2 * quarter, pairs))
    z_sum()
    loop(forward_pair, min(2 * quarter, pairs), min(3 * quarter, pairs))
    grads_start()
    loop(forward_pair, min(3 * quarter, pairs), pairs)
    row2_copy.wait()
    mean2[...] = down((row2_out[...] + row2_in[...]) / dim)

    def ig_copy(c):
        return pltpu.make_async_copy(ig_v.at[c], ig_h.at[:, lanes(c)], out_sem.at[1, c])

    def finish(c):
        inv = both(inv_rms[...])
        normed = act[c].astype(F32) * inv
        ig_v[c] = (inv * (f_ext[c, :rows, :] - normed * both(mean2[...]))).astype(BF16)
        ig_copy(c).start()

    loop(finish)

    def half_copy(i, k):
        half = mr_all.at[i, k]
        return remote(half, half, cg_send.at[i], cg_recv.at[i], other_core)

    def mr_copy(c):
        return pltpu.make_async_copy(
            mr_all.at[c // 2, lax.rem(c, 2), pl.ds(0, BLK), :], mr_h.at[:, lanes(c)], out_sem.at[2, c]
        )

    def spread(c):
        mr_copy(c).start()
        x = mr_all[c // 2, lax.rem(c, 2), BLK:, :].astype(F32)
        x = x[:8] + x[8:]
        seg_ref[:, lanes(c)] = x[:SE]
        gg_ref[:, lanes(c)] = x[SE:]

    def arrived(i):
        @pl.when(i != xy)
        def _():
            xg_copy(i, i).wait_recv()

        half_copy(i, core).start()

    loop(arrived, 0, pairs)
    loop(lambda i: spread(2 * i + core), 0, pairs)

    def across_cores(i):
        half_copy(i, core).wait_send()
        half_copy(i, 1 - core).wait_recv()
        spread(2 * i + 1 - core)

    loop(across_cores, 0, pairs)

    for d in range(1, pn):
        p = lax.rem(xy + d, pn)
        xy_copy(p).wait_send()
        xg_copy(xy, p).wait_send()
    for d in range(1, zn):
        z_copy(lax.rem(z + d, zn)).wait_send()

    def drain(c):
        g_copy(c).wait_send()
        head_copy(c).wait_send()
        out_copy(c).wait()
        ig_copy(c).wait()
        mr_copy(c).wait()

    loop(drain)


def hand_over(*arrays):
    count = len(arrays)

    def body(*refs):
        sems = refs[-1]
        loads, stores = [], []
        for src, dst, via, x in zip(refs, refs[count:], refs[2 * count :], arrays):
            parts = x.shape[0] // 64 or 1
            size = x.shape[0] // parts
            for p in range(parts):
                at, n = pl.ds(p * size, size), len(loads)
                loads.append(pltpu.make_async_copy(src.at[at], via.at[at], sems.at[0, n]))
                stores.append(pltpu.make_async_copy(via.at[at], dst.at[at], sems.at[1, n]))
        for load in loads:
            load.start()
        for load, store in zip(loads, stores):
            load.wait()
            store.start()
        for store in stores:
            store.wait()

    any_spec = pl.BlockSpec(memory_space=pl.ANY)
    return pl.pallas_call(
        body,
        out_shape=[jax.ShapeDtypeStruct(x.shape, x.dtype) for x in arrays],
        in_specs=[any_spec] * count,
        out_specs=[any_spec] * count,
        scratch_shapes=[pltpu.VMEM(x.shape, x.dtype) for x in arrays] + [pltpu.SemaphoreType.DMA((2, 16))],
        compiler_params=pltpu.CompilerParams(vmem_limit_bytes=60 * 1024 * 1024),
        name="hand_over",
    )(*arrays)


def per_device(seq_size, dim, tokens, act, gain, gate, se, mrf, off, cot):
    rows, chans = act.shape
    nc = chans // CH
    zn = 8 if seq_size == 128 else 2
    pn = seq_size // (2 * zn)
    assert nc == 2 * pn and rows == 2 * BLK and mrf.shape[0] == BLK and se.shape[0] == SE
    fwd, inv_hi, inv_lo = transforms()
    any_spec = pl.BlockSpec(memory_space=pl.ANY)
    vmem = pl.BlockSpec(memory_space=pltpu.VMEM)
    smem = pl.BlockSpec(memory_space=pltpu.SMEM)
    part = BLK // zn
    scratch = [
        ((nc, rows, CH), BF16), ((nc, rows, CH), BF16), ((nc, rows, CH), BF16), ((nc, BLK, CH), BF16),
        ((nc, rows, CH), BF16), ((nc, rows, CH), BF16), ((nc, rows, CH), BF16), ((nc, rows, CH), BF16), ((rows, CH), BF16),
        ((nc, rows, CH), BF16), ((nc, rows + 8, CH), F32), ((nc, 8, CH), F32), ((nc, 8, CH), F32),
        ((nc, rows + 8, CH), F32), ((nc, 8, CH), F32), ((nc, rows, CH), F32),
        ((nc, rows, CH), BF16), ((nc, rows, CH), BF16), ((rows, BLK), F32), ((8, rows), F32), ((8, rows), F32),
        ((rows, BLK), F32), ((8, rows), F32), ((8, rows), F32), ((8, CH), F32), ((rows, BLK), F32),
        ((nc, LAGS, CH), F32), ((pn, LAGS, CH), F32), ((pn, LAGS + 8, CH), BF16), ((pn, LAGS + 8, CH), BF16),
        ((LAGS, CH), F32), ((zn, part, CH), F32), ((zn, part, CH), F32), ((8, CH), F32), ((zn, 8, CH), F32), ((LAGS, CH), F32),
        ((pn, 2, LAGS + 8, CH), BF16),
    ]
    sems = [(4, nc), (3, nc), nc, nc, nc, nc, 1, 1, nc, nc, 2, 2, pn, pn, pn, pn, zn, zn, 1, zn, zn, zn, zn, 1, pn, pn, pn, pn]
    sems = [pltpu.SemaphoreType.DMA(s if isinstance(s, tuple) else (s,)) for s in sems]
    out, ig, gg, seg, mr = pl.pallas_call(
        functools.partial(kernel, pn, zn, seq_size, dim, 1.0 / math.sqrt(tokens)),
        out_shape=(
            jax.ShapeDtypeStruct((rows, chans), BF16),
            jax.ShapeDtypeStruct((rows, chans), BF16),
            jax.ShapeDtypeStruct((1, chans), F32),
            jax.ShapeDtypeStruct((SE, chans), F32),
            jax.ShapeDtypeStruct((BLK, chans), BF16),
        ),
        in_specs=[any_spec, vmem, any_spec, vmem, any_spec, smem, any_spec, vmem, vmem, vmem],
        out_specs=(any_spec, any_spec, vmem, vmem, any_spec),
        scratch_shapes=[pltpu.VMEM(*s) for s in scratch] + sems,
        compiler_params=pltpu.CompilerParams(
            collective_id=0, has_side_effects=True, vmem_limit_bytes=58 * 1024 * 1024
        ),
        name="hyena",
    )(act, gain.reshape(1, chans), gate, se, mrf, off, cot, fwd, inv_hi, inv_lo)
    out, ig, gg, seg, mr = hand_over(out, ig, gg, seg, mr)
    return out, ig, gg.reshape(chans), seg, mr


def solution(mesh):
    in_specs = (
        P("seq", "tp"), P("tp"), P("seq", "tp"), P(None, "tp"), P(None, "tp"), P("tp"), P("seq", "tp"),
    )
    out_specs = (P("seq", "tp"), P("seq", "tp"), P("tp"), P(None, "tp"), P(None, "tp"))

    def whole(act, *rest):
        tokens, dim = act.shape
        body = functools.partial(per_device, mesh.shape["seq"], dim, tokens)
        return jax.shard_map(
            body, mesh=mesh, in_specs=in_specs, out_specs=out_specs, check_vma=False
        )(act, *rest)

    return whole
```

```python
import functools
import math

import jax
import jax.numpy as jnp
import numpy as np
from jax import lax
from jax.experimental import pallas as pl
from jax.experimental.pallas import tpu as pltpu
from jax.sharding import PartitionSpec as P

MESH = pl.DeviceIdType.MESH
CH = 256
BLK = 128
SE = 7
LAGS = BLK + 8
NEAR = BLK + 16
F32 = jnp.float32
BF16 = jnp.bfloat16


def transforms():
    angle = np.pi * (2 * np.arange(BLK)[:, None] + 1) * np.arange(2 * BLK)[None, :] / (2 * BLK)
    forward = np.concatenate([np.cos(angle), -np.sin(angle)], axis=0)
    inverse = forward.T / BLK
    return (
        jnp.asarray(forward, BF16),
        jnp.asarray(inverse[BLK:], BF16),
        jnp.asarray(np.concatenate([inverse[:LAGS], inverse[:LAGS]], axis=1), BF16),
    )


def dot(a, b):
    return jnp.dot(a, b, preferred_element_type=F32)


def remote(src, dst, send_sem, recv_sem, device):
    return pltpu.make_async_remote_copy(
        src_ref=src, dst_ref=dst, send_sem=send_sem, recv_sem=recv_sem,
        device_id=device, device_id_type=MESH,
    )


def both(x):
    return jnp.concatenate([x, x], axis=1)


def split(x):
    top = x.astype(BF16)
    return top, (x - top.astype(F32)).astype(BF16)


def kernel(
    pn, zn, seq_size, dim, scale,
    act_h, gain_ref, gate_h, se_ref, mrf_h, off_ref, cot_h, fwd_ref, inv_hi_ref, inv_lo_ref,
    out_h, ig_h, gg_ref, seg_ref, mr_h,
    act, gate, cot, mrf, g_own, g_halo, f_own, f_halo, zeros, tail, ext, scaled, b_ext, head_in, spec,
    out_v, ig_v, row_acc, row_out, row_in, inv_rms, row2_out, row2_in, no_rows, mean2,
    red, core_in, xy_out, xy_in, own_sum, z_out, z_in, z_last_out, z_last_in, lags, mr_all,
    in_sem, out_sem, g_send, g_recv, f_send, f_recv, tail_send, tail_recv, head_send, head_recv, row_send, row_recv,
    core_send, core_recv, xy_send, xy_recv, z_send, z_recv, zl_send, zl_recv, zg_send, zg_recv, zgl_send, zgl_recv, xg_send, xg_recv, cg_send, cg_recv,
):
    nc = act.shape[0]
    rows = act.shape[1]
    seq = lax.axis_index("seq")
    tp = lax.axis_index("tp")
    core = lax.rem(seq, 2)
    z = lax.rem(seq // 2, zn)
    xy = seq // (2 * zn)
    first = seq == 0
    last = seq == seq_size - 1
    after = (lax.rem(seq + 1, seq_size), tp)
    before = (lax.rem(seq + seq_size - 1, seq_size), tp)
    pair = (seq, 1 - tp)
    other_core = (seq + 1 - 2 * core, tp)

    def xy_peer(p):
        return (p * (2 * zn) + z * 2 + core, tp)

    def z_peer(j):
        return (xy * (2 * zn) + j * 2 + core, tp)

    def turn(start, t):
        return lax.rem(start + pn - t, pn)

    before_xy = lax.rem(seq + seq_size - 1, seq_size) // (2 * zn)
    after_xy = lax.rem(seq + 1, seq_size) // (2 * zn)

    def lanes(c):
        return pl.ds(pl.multiple_of(c * CH, CH), CH)

    def in_copy(n, c):
        src, dst = ((act_h, act), (gate_h, gate), (cot_h, cot), (mrf_h, mrf))[n]
        return pltpu.make_async_copy(src.at[:, lanes(c)], dst.at[c], in_sem.at[n, c])

    def loop(body, start=0, stop=nc):
        def step(c, carry):
            body(c)
            return carry

        lax.fori_loop(start, stop, step, 0)

    barrier = pltpu.get_barrier_semaphore()
    partners = [after, before, pair, other_core]
    partners += [xy_peer(lax.rem(xy + d, pn)) for d in range(1, pn)]
    partners += [z_peer(lax.rem(z + d, zn)) for d in range(1, zn)]
    for partner in partners:
        pl.semaphore_signal(barrier, inc=1, device_id=partner, device_id_type=MESH)

    def fetch(t):
        i = turn(before_xy, t)
        for c in (2 * i, 2 * i + 1):
            in_copy(1, c).start()
            in_copy(2, c).start()

    pairs = nc // 2
    loop(lambda c: in_copy(0, c).start())
    loop(fetch, 0, pairs)
    loop(lambda c: in_copy(3, c).start())

    zeros[...] = jnp.zeros_like(zeros)
    no_rows[...] = jnp.zeros_like(no_rows)
    row_acc[...] = jnp.zeros_like(row_acc)

    def squares(c):
        in_copy(0, c).wait()
        a = act[c].astype(F32)
        a = a * a
        row_acc[...] += a[:, :BLK] + a[:, BLK:]

    def across(acc):
        return jnp.broadcast_to(jnp.sum(jnp.transpose(acc), axis=0, keepdims=True), (8, rows))

    def down(x):
        return jnp.broadcast_to(jnp.transpose(x)[:, :1], (rows, BLK))

    pl.semaphore_wait(barrier, len(partners))

    loop(squares)
    row_out[...] = across(row_acc[...])
    row_copy = remote(row_out, row_in, row_send.at[0], row_recv.at[0], pair)
    row_copy.start()

    def g_copy(n, c, src=None):
        at = pl.ds(n * NEAR, rows - NEAR if n else NEAR)
        src = g_own.at[c, at, :] if src is None else src.at[at, :]
        return remote(src, g_halo.at[c, at, :], g_send.at[n, c], g_recv.at[n, c], before)

    def g_start(n, c):
        @pl.when(first)
        def _():
            g_copy(n, c, zeros).start()

        @pl.when(jnp.logical_not(first))
        def _():
            g_copy(n, c).start()

    def gated_pair(t):
        i = turn(before_xy, t)
        for c in (2 * i, 2 * i + 1):
            in_copy(1, c).wait()
            in_copy(2, c).wait()
            g_own[c] = (cot[c].astype(F32) * gate[c].astype(F32)).astype(BF16)
            g_start(0, c)

    loop(gated_pair, 0, pairs)
    loop(lambda c: g_start(1, c))

    def filtered(i):
        for n in range(4):
            in_copy(3, 4 * i + n).wait()
        for n in range(4):
            spec[4 * i + n] = dot(fwd_ref[:, :BLK], mrf[4 * i + n])

    loop(filtered, 0, nc // 4)

    row_copy.wait()
    inv_rms[...] = down(lax.rsqrt((row_out[...] + row_in[...]) / dim + 1e-06))

    def f_copy(n, c, src=None):
        at = pl.ds(n * BLK, BLK)
        src = f_own.at[c, at, :] if src is None else src.at[at, :]
        return remote(src, f_halo.at[c, at, :], f_send.at[n, c], f_recv.at[n, c], after)

    def f_start(n, c):
        @pl.when(last)
        def _():
            f_copy(n, c, zeros).start()

        @pl.when(jnp.logical_not(last))
        def _():
            f_copy(n, c).start()

    def featured_pair(t):
        i = turn(after_xy, t)
        for c in (2 * i, 2 * i + 1):
            f_own[c] = (act[c].astype(F32) * both(inv_rms[...]) * gain_ref[:, lanes(c)]).astype(BF16)
            f_start(1, c)

    loop(featured_pair, 0, pairs)
    loop(lambda c: f_start(0, c))

    def upper(c):
        left = jnp.full((BLK, BLK), off_ref[2 * c], jnp.int32)
        right = jnp.full((BLK, BLK), off_ref[2 * c + 1], jnp.int32)
        return jnp.concatenate([left, right], axis=1).astype(F32)

    def lag_sums(c):
        flag = upper(c)
        up = flag.astype(BF16) > 0.5
        g0, g1, g2 = g_own[c, :BLK], g_own[c, BLK:], g_halo[c, :BLK]
        fm, f0, f1 = f_halo[c, BLK:], f_own[c, :BLK], f_own[c, BLK:]
        kr, ki = 0.0, 0.0
        for window, f in (((g0, g1), jnp.where(up, fm, f0)), ((g1, g2), jnp.where(up, f0, f1))):
            v = dot(fwd_ref[...], jnp.concatenate(window, axis=0))
            s = dot(fwd_ref[:, :BLK], f)
            vr, vi, sr, si = v[:BLK], v[BLK:], s[:BLK], s[BLK:]
            kr = kr + (sr * vr + si * vi)
            ki = ki + (sr * vi - si * vr)
        top, low = split(jnp.concatenate([kr, ki], axis=0))
        x = dot(inv_lo_ref[...], jnp.concatenate([top, low], axis=0))
        red[c, :BLK, :] = x[:BLK]
        up8 = flag[:8] > 0.5
        em, e0, e1 = (f[BLK - 16 :].astype(F32)[8:] for f in (fm, f0, f1))
        fa, fb = jnp.where(up8, em, e0), jnp.where(up8, e0, e1)
        ua = g0[:16].astype(F32)[:8] + g2[:16].astype(F32)[:8]
        ub = g1[:16].astype(F32)[:8] + g_halo[c, BLK:NEAR].astype(F32)[:8]
        row = lax.broadcasted_iota(jnp.int32, (8, CH), 0)
        fix = x[BLK:]
        for r in range(1, SE - 1):
            term = pltpu.roll(fa, r, 0) * ua + pltpu.roll(fb, r, 0) * ub
            term = jnp.sum(jnp.where(row < r, term, 0.0), axis=0, keepdims=True)
            fix = fix + jnp.where(row == r, term, 0.0)
        red[c, BLK:, :] = fix

    def backward(c):
        up = upper(c).astype(BF16) > 0.5
        g0, g1 = g_own[c, :BLK], g_own[c, BLK:]
        g2, g3 = g_halo[c, :BLK], g_halo[c, BLK:]
        v0, v1, v2 = jnp.where(up, g1, g0), jnp.where(up, g2, g1), jnp.where(up, g3, g2)
        hr, hi = spec[c, :BLK], spec[c, BLK:]
        for n, window in enumerate(((v0, v1), (v1, v2))):
            v = dot(fwd_ref[...], jnp.concatenate(window, axis=0))
            vr, vi = v[:BLK], v[BLK:]
            prod = jnp.concatenate([hr * vr + hi * vi, hr * vi - hi * vr], axis=0).astype(BF16)
            b_ext[c, n * BLK : (n + 1) * BLK, :] = dot(inv_lo_ref[:BLK, : 2 * BLK], prod)

    def head_copy(c, src=None):
        src = b_ext.at[c, pl.ds(0, 8), :] if src is None else src
        return remote(src, head_in.at[c], head_send.at[c], head_recv.at[c], before)

    def core_copy(i):
        return remote(red.at[2 * i + 1 - core], core_in.at[i], core_send.at[i], core_recv.at[i], other_core)

    def lag_pair(t):
        i = turn(xy, t)
        for c in (2 * i, 2 * i + 1):
            g_copy(0, c).wait_recv()
            f_copy(1, c).wait_recv()
        for c in (2 * i, 2 * i + 1):
            lag_sums(c)
        core_copy(i).start()

    def backward_pair(i):
        for c in (2 * i, 2 * i + 1):
            g_copy(1, c).wait_recv()
        for c in (2 * i, 2 * i + 1):
            backward(c)
        for c in (2 * i, 2 * i + 1):

            @pl.when(first)
            def _(c=c):
                head_copy(c, no_rows).start()

            @pl.when(jnp.logical_not(first))
            def _(c=c):
                head_copy(c).start()

    def back_short(c):
        b_ext[c, rows:, :] = head_in[c]
        taps = se_ref[:, lanes(c)]
        gain = gain_ref[:, lanes(c)]
        for r in range(0, rows, 64):
            at = slice(r, r + 64)
            grad = taps[0:1] * b_ext[c, at, :]
            for k in range(1, SE):
                grad = grad + taps[k : k + 1] * b_ext[c, r + k : r + k + 64, :]
            grad = grad * gain
            inner = grad * (act[c, at].astype(F32) * both(inv_rms[at]))
            row_acc[at] += inner[:, :BLK] + inner[:, BLK:]
            scaled[c, at, :] = grad

    def back_short_pair(i):
        for c in (2 * i, 2 * i + 1):
            head_copy(c).wait()
        for c in (2 * i, 2 * i + 1):
            back_short(c)

    def xy_copy(p):
        return remote(xy_out.at[p], xy_in.at[xy], xy_send.at[p], xy_recv.at[xy], xy_peer(p))

    def xy_start(t):
        i = turn(xy, t)
        core_copy(i).wait()
        q = red[2 * i + core] + core_in[i]

        @pl.when(i == xy)
        def _():
            own_sum[...] = q

        @pl.when(i != xy)
        def _():
            xy_out[i, :BLK, :] = q[:BLK].astype(BF16)
            top = q[BLK:].astype(BF16).astype(F32)
            xy_out[i, BLK:, :] = jnp.concatenate([top, q[BLK:] - top], axis=0).astype(BF16)
            xy_copy(i).start()

    def out_copy(c):
        return pltpu.make_async_copy(out_v.at[c], out_h.at[:, lanes(c)], out_sem.at[0, c])

    def forward(c, n):
        flag = upper(c)
        up = flag.astype(BF16) > 0.5
        fl, fm, f0, f1 = f_halo[c, :BLK], f_halo[c, BLK:], f_own[c, :BLK], f_own[c, BLK:]
        ext[n, :8, :] = jnp.where(flag[:8] > 0.5, tail[c].astype(F32)[8:], fl[BLK - 16 :].astype(F32)[8:])
        for b, f in enumerate((jnp.where(up, fl, fm), jnp.where(up, fm, f0), jnp.where(up, f0, f1))):
            ext[n, 8 + b * BLK : 8 + (b + 1) * BLK, :] = f.astype(F32)
        taps = se_ref[:, lanes(c)]
        short = []
        for r in range(8, 8 + 3 * BLK, 64):
            total = taps[0:1] * ext[n, r : r + 64, :]
            for k in range(1, SE):
                total = total + taps[k : k + 1] * ext[n, r - k : r + 64 - k, :]
            short.append(total.astype(BF16))
        hr, hi = spec[c, :BLK], spec[c, BLK:]
        for b in range(2):
            at = slice(b * BLK, (b + 1) * BLK)
            w = dot(fwd_ref[...], jnp.concatenate(short[2 * b : 2 * b + 4], axis=0))
            wr, wi = w[:BLK], w[BLK:]
            prod = jnp.concatenate([hr * wr - hi * wi, hr * wi + hi * wr], axis=0).astype(BF16)
            y = dot(inv_hi_ref[...], prod)
            out_v[c, at] = (gate[c, at].astype(F32) * y).astype(BF16)

    def forward_pair(i):
        for c in (2 * i, 2 * i + 1):
            f_copy(0, c).wait_recv()
        for n in range(2):
            forward(2 * i + n, n)
        for c in (2 * i, 2 * i + 1):
            out_copy(c).start()

    part = BLK // zn
    end = zn - 1

    def z_copy(j):
        return remote(z_out.at[j], z_in.at[z], z_send.at[j], z_recv.at[z], z_peer(j))

    def z_last_copy():
        return remote(z_last_out, z_last_in.at[z], zl_send.at[0], zl_recv.at[z], z_peer(end))

    def z_start():
        for d in range(1, pn):
            p = lax.rem(xy + d, pn)
            remote(xy_out.at[p], xy_in.at[p], xy_send.at[p], xy_recv.at[p], xy_peer(p)).wait_recv()
        total = own_sum[...]
        for d in range(1, pn):
            x = xy_in[lax.rem(xy + d, pn)].astype(F32)
            total = total + jnp.concatenate([x[:BLK], x[BLK : BLK + 8] + x[BLK + 8 :]], axis=0)
        for j in range(zn):
            z_out[j] = total[j * part : (j + 1) * part]
        z_last_out[...] = total[BLK:]
        for d in range(1, zn):
            z_copy(lax.rem(z + d, zn)).start()

        @pl.when(z != end)
        def _():
            z_last_copy().start()

    def piece(j):
        return lags.at[pl.ds(pl.multiple_of(j * part, part), part), :]

    def zg_copy(i, j):
        return remote(piece(i), piece(i), zg_send.at[j], zg_recv.at[i], z_peer(j))

    def zg_last_copy(j):
        rest = lags.at[pl.ds(BLK, 8), :]
        return remote(rest, rest, zgl_send.at[j], zgl_recv.at[0], z_peer(j))

    def z_sum():
        total = z_out[z]
        for d in range(1, zn):
            j = lax.rem(z + d, zn)
            remote(z_out.at[j], z_in.at[j], z_send.at[j], z_recv.at[j], z_peer(j)).wait_recv()
            total = total + z_in[j]
        lags[pl.ds(pl.multiple_of(z * part, part), part), :] = total
        for d in range(1, zn):
            zg_copy(z, lax.rem(z + d, zn)).start()

        @pl.when(z == end)
        def _():
            rest = z_last_out[...]
            for j in range(zn - 1):
                remote(z_last_out, z_last_in.at[j], zl_send.at[0], zl_recv.at[j], z_peer(j)).wait_recv()
                rest = rest + z_last_in[j]
            lags[BLK:, :] = rest
            for j in range(zn - 1):
                zg_last_copy(j).start()

    def xg_copy(p, q):
        half = mr_all.at[p, core]
        return remote(half, half, xg_send.at[q], xg_recv.at[p], xy_peer(q))

    def grads_start():
        for d in range(1, zn):
            j = lax.rem(z + d, zn)
            zg_copy(z, j).wait_send()
            zg_copy(j, j).wait_recv()

        @pl.when(z != end)
        def _():
            z_last_copy().wait_send()
            zg_last_copy(end).wait_recv()

        @pl.when(z == end)
        def _():
            for j in range(zn - 1):
                zg_last_copy(j).wait_send()

        mine = 2 * xy + core
        taps = se_ref[:, lanes(mine)]
        filt = mrf[mine].astype(F32)
        grads = []
        kern = jnp.zeros((BLK, CH), F32)
        gain_sum = jnp.zeros((1, CH), F32)
        for k in range(SE):
            x = lags[k : k + BLK, :]
            kern = kern + taps[k : k + 1] * x
            grads.append(jnp.sum(filt * x, axis=0, keepdims=True) * scale)
            gain_sum = gain_sum + taps[k : k + 1] * grads[k]
        grads.append(gain_sum / gain_ref[:, lanes(mine)])
        grads = jnp.concatenate(grads, axis=0)
        top = grads.astype(BF16).astype(F32)
        mr_all[xy, core, :BLK, :] = (kern * scale).astype(BF16)
        mr_all[xy, core, BLK:, :] = jnp.concatenate([top, grads - top], axis=0).astype(BF16)
        for d in range(1, pn):
            xg_copy(xy, lax.rem(xy + d, pn)).start()

    def first_lags(t):
        lag_pair(t)

    def lags_and_sums(t):
        lag_pair(t)
        xy_start(t - 1)

    loop(first_lags, 0, 1)
    loop(lags_and_sums, 1, pairs)
    tail_copy = remote(
        f_halo.at[:, pl.ds(rows - 16, 16), :], tail, tail_send.at[0], tail_recv.at[0], after
    )
    tail_copy.start()
    xy_start(pairs - 1)

    half = pairs // 2
    row_acc[...] = jnp.zeros_like(row_acc)
    loop(backward_pair, 0, pairs)
    loop(back_short_pair, 0, pairs)
    row2_out[...] = across(row_acc[...])
    row2_copy = remote(row2_out, row2_in, row_send.at[1], row_recv.at[1], pair)
    row2_copy.start()
    tail_copy.wait()

    @pl.when(first)
    def _():
        tail[...] = jnp.zeros_like(tail)

    z_start()
    loop(forward_pair, 0, half)
    z_sum()
    row2_copy.wait()
    mean2[...] = down((row2_out[...] + row2_in[...]) / dim)

    def ig_copy(c):
        return pltpu.make_async_copy(ig_v.at[c], ig_h.at[:, lanes(c)], out_sem.at[1, c])

    def finish(c):
        inv = both(inv_rms[...])
        normed = act[c].astype(F32) * inv
        ig_v[c] = (inv * (scaled[c] - normed * both(mean2[...]))).astype(BF16)
        ig_copy(c).start()

    loop(finish)
    grads_start()
    loop(forward_pair, half, pairs)

    def half_copy(i, k):
        half = mr_all.at[i, k]
        return remote(half, half, cg_send.at[i], cg_recv.at[i], other_core)

    def mr_copy(c):
        return pltpu.make_async_copy(
            mr_all.at[c // 2, lax.rem(c, 2), pl.ds(0, BLK), :], mr_h.at[:, lanes(c)], out_sem.at[2, c]
        )

    def spread(c):
        mr_copy(c).start()
        x = mr_all[c // 2, lax.rem(c, 2), BLK:, :].astype(F32)
        x = x[:8] + x[8:]
        seg_ref[:, lanes(c)] = x[:SE]
        gg_ref[:, lanes(c)] = x[SE:]

    def arrived(i):
        @pl.when(i != xy)
        def _():
            xg_copy(i, i).wait_recv()

        half_copy(i, core).start()

    loop(arrived, 0, pairs)
    loop(lambda i: spread(2 * i + core), 0, pairs)

    def across_cores(i):
        half_copy(i, core).wait_send()
        half_copy(i, 1 - core).wait_recv()
        spread(2 * i + 1 - core)

    loop(across_cores, 0, pairs)

    for d in range(1, pn):
        p = lax.rem(xy + d, pn)
        xy_copy(p).wait_send()
        xg_copy(xy, p).wait_send()
    for d in range(1, zn):
        z_copy(lax.rem(z + d, zn)).wait_send()

    def drain(c):
        for n in range(2):
            g_copy(n, c).wait_send()
            f_copy(n, c).wait_send()
        out_copy(c).wait()
        ig_copy(c).wait()
        mr_copy(c).wait()

    loop(drain)


def hand_over(*arrays):
    count = len(arrays)

    def body(*refs):
        sems = refs[-1]
        loads, stores = [], []
        for src, dst, via, x in zip(refs, refs[count:], refs[2 * count :], arrays):
            parts = x.shape[0] // 64 or 1
            size = x.shape[0] // parts
            for p in range(parts):
                at, n = pl.ds(p * size, size), len(loads)
                loads.append(pltpu.make_async_copy(src.at[at], via.at[at], sems.at[0, n]))
                stores.append(pltpu.make_async_copy(via.at[at], dst.at[at], sems.at[1, n]))
        for load in loads:
            load.start()
        for load, store in zip(loads, stores):
            load.wait()
            store.start()
        for store in stores:
            store.wait()

    any_spec = pl.BlockSpec(memory_space=pl.ANY)
    return pl.pallas_call(
        body,
        out_shape=[jax.ShapeDtypeStruct(x.shape, x.dtype) for x in arrays],
        in_specs=[any_spec] * count,
        out_specs=[any_spec] * count,
        scratch_shapes=[pltpu.VMEM(x.shape, x.dtype) for x in arrays] + [pltpu.SemaphoreType.DMA((2, 16))],
        compiler_params=pltpu.CompilerParams(vmem_limit_bytes=60 * 1024 * 1024),
        name="hand_over",
    )(*arrays)


def per_device(seq_size, dim, tokens, act, gain, gate, se, mrf, off, cot):
    rows, chans = act.shape
    nc = chans // CH
    zn = 8 if seq_size == 128 else 2
    pn = seq_size // (2 * zn)
    assert nc == 2 * pn and rows == 2 * BLK and mrf.shape[0] == BLK and se.shape[0] == SE
    fwd, inv_hi, inv_lo = transforms()
    any_spec = pl.BlockSpec(memory_space=pl.ANY)
    vmem = pl.BlockSpec(memory_space=pltpu.VMEM)
    smem = pl.BlockSpec(memory_space=pltpu.SMEM)
    part = BLK // zn
    scratch = [
        ((nc, rows, CH), BF16), ((nc, rows, CH), BF16), ((nc, rows, CH), BF16), ((nc, BLK, CH), BF16),
        ((nc, rows, CH), BF16), ((nc, rows, CH), BF16), ((nc, rows, CH), BF16), ((nc, rows, CH), BF16), ((rows, CH), BF16),
        ((nc, 16, CH), BF16), ((2, 3 * BLK + 8, CH), F32), ((nc, rows, CH), F32), ((nc, rows + 8, CH), F32),
        ((nc, 8, CH), F32), ((nc, rows, CH), F32),
        ((nc, rows, CH), BF16), ((nc, rows, CH), BF16), ((rows, BLK), F32), ((8, rows), F32), ((8, rows), F32),
        ((rows, BLK), F32), ((8, rows), F32), ((8, rows), F32), ((8, CH), F32), ((rows, BLK), F32),
        ((nc, LAGS, CH), F32), ((pn, LAGS, CH), F32), ((pn, LAGS + 8, CH), BF16), ((pn, LAGS + 8, CH), BF16),
        ((LAGS, CH), F32), ((zn, part, CH), F32), ((zn, part, CH), F32), ((8, CH), F32), ((zn, 8, CH), F32), ((LAGS, CH), F32),
        ((pn, 2, LAGS + 8, CH), BF16),
    ]
    sems = [(4, nc), (3, nc), (2, nc), (2, nc), (2, nc), (2, nc), 1, 1, nc, nc, 2, 2, pn, pn, pn, pn, zn, zn, 1, zn, zn, zn, zn, 1, pn, pn, pn, pn]
    sems = [pltpu.SemaphoreType.DMA(s if isinstance(s, tuple) else (s,)) for s in sems]
    out, ig, gg, seg, mr = pl.pallas_call(
        functools.partial(kernel, pn, zn, seq_size, dim, 1.0 / math.sqrt(tokens)),
        out_shape=(
            jax.ShapeDtypeStruct((rows, chans), BF16),
            jax.ShapeDtypeStruct((rows, chans), BF16),
            jax.ShapeDtypeStruct((1, chans), F32),
            jax.ShapeDtypeStruct((SE, chans), F32),
            jax.ShapeDtypeStruct((BLK, chans), BF16),
        ),
        in_specs=[any_spec, vmem, any_spec, vmem, any_spec, smem, any_spec, vmem, vmem, vmem],
        out_specs=(any_spec, any_spec, vmem, vmem, any_spec),
        scratch_shapes=[pltpu.VMEM(*s) for s in scratch] + sems,
        compiler_params=pltpu.CompilerParams(
            collective_id=0, has_side_effects=True, vmem_limit_bytes=58 * 1024 * 1024
        ),
        name="hyena",
    )(act, gain.reshape(1, chans), gate, se, mrf, off, cot, fwd, inv_hi, inv_lo)
    out, ig, gg, seg, mr = hand_over(out, ig, gg, seg, mr)
    return out, ig, gg.reshape(chans), seg, mr


def solution(mesh):
    in_specs = (
        P("seq", "tp"), P("tp"), P("seq", "tp"), P(None, "tp"), P(None, "tp"), P("tp"), P("seq", "tp"),
    )
    out_specs = (P("seq", "tp"), P("seq", "tp"), P("tp"), P(None, "tp"), P(None, "tp"))

    def whole(act, *rest):
        tokens, dim = act.shape
        body = functools.partial(per_device, mesh.shape["seq"], dim, tokens)
        return jax.shard_map(
            body, mesh=mesh, in_specs=in_specs, out_specs=out_specs, check_vma=False
        )(act, *rest)

    return whole
```
